32 devices in a mesh: runs: 2 (over y), blk: 4 (over z), term: 4 (over x, core).
Axes of the slice: x: 2, y: 2, z: 4, core: 2. Of those that a mesh axis runs over, the one named last changes fastest.
Arguments:
- two_site: bfloat16 [8, 4, 256, 256], P(('runs', 'blk')), parts along dimension 0, may hold values from -6 to 6
- left_env: bfloat16 [8, 4, 256, 256], P(('runs', 'term'), 'blk'), parts along dimension 0, may hold values from -0.375 to 0.375
- right_env: bfloat16 [8, 4, 256, 256], P(('runs', 'term'), 'blk'), parts along dimension 0, may hold values from -0.375 to 0.375
- row_size: int32 [8], P(('runs', 'blk')), parts along dimension 0, may hold values from 64 to 256
- col_size: int32 [8], P('runs'), parts along dimension 0, may hold values from 64 to 256
- block_live: int32 [8, 4], P(('runs', 'blk')), parts along dimension 0, may hold values 0 or 1
Outputs:
- first_image: bfloat16 [8, 4, 256, 256], P(('runs', 'blk'), 'term'), parts along dimension 0
- second_image: bfloat16 [8, 4, 256, 256], P(('runs', 'blk'), 'term'), parts along dimension 0
The draws below stay inside these ranges and needn't reach their ends.
There are 2 independent parts, one for each index of `runs`. The reference program is written for one: setup_inputs(seed, part) draws one part's arguments, and reference() takes and returns one part's arrays. A program takes and returns all parts, laid end to end along the dimension named above; each array names one. Nothing has to cross between parts.
All inputs are finite; a program needn't handle non-finite values. No bound on the sum of `block_live` on one device may be relied on, other than what follows from the above.
Results may differ from the reference program's by a relative error of at most 0.029.
Values may be sent and summed in bfloat16 or wider, within the bound.
No kernel may reach another device: no remote copies, remote signals or barrier semaphores. Data moves between devices by JAX's collectives and lax.ppermute only.
A program may use at most 64 MiB of HBM per device.

```python
import jax
import jax.numpy as jnp
from jax import lax

M = 256
NL = 4
NR = 4
TERMS = 4


def place_ends(drawn, key, least, top_value):
    extent = drawn.shape
    index_at = [jax.random.randint(jax.random.fold_in(key, axis), (), 0, extent[axis]) for axis in range(len(extent))]
    drawn = drawn.at[tuple(index_at)].set(least)
    longest = extent.index(max(extent))
    index_at[longest] = (index_at[longest] + 1) % extent[longest]
    return drawn.at[tuple(index_at)].set(top_value)


def block_levels(key, dims, split, low, largest):
    def one(position, parts):
        draws = jax.random.uniform(jax.random.fold_in(jax.random.fold_in(key, 6), position), (parts,), jnp.float32, low / len(split), largest / len(split))
        return jnp.repeat(jnp.exp(draws), dims[position] // parts).reshape((-1,) + (1,) * (len(dims) - position - 1))

    loudness = one(*split[0])
    for cut in split[1:]:
        loudness = loudness * one(*cut)
    return loudness


def centred(stream_key, extent, width, reach, pieces=(), held_as=jnp.bfloat16):
    factor_of = block_levels(stream_key, extent, pieces, -0.22, 0.18) if pieces else 1.0
    values = jax.random.normal(stream_key, extent, jnp.float32) * width * factor_of
    return jnp.minimum(jnp.maximum(values, -reach), reach).astype(held_as)


def setup_inputs(seed: int = 0, part: int = 0) -> dict:
    keys = jax.random.split(jax.random.key(seed), 7)
    part_keys = jax.random.split(jax.random.fold_in(keys[6], part), 7)
    return {
        "two_site": centred(part_keys[0], (NL, NR, M, M), 1.0, 6.0, ((0, 4),)),
        "left_env": centred(part_keys[1], (TERMS, NL, M, M), M ** -0.5, 0.375, ((0, 4), (1, 4))),
        "right_env": centred(part_keys[2], (TERMS, NR, M, M), M ** -0.5, 0.375, ((0, 4), (1, 4))),
        "row_size": place_ends(jax.random.randint(part_keys[3], (NL,), M // 4, M + 1), jax.random.fold_in(part_keys[3], 1), M // 4, M).astype(jnp.int32),
        "col_size": place_ends(jax.random.randint(part_keys[4], (NR,), M // 4, M + 1), jax.random.fold_in(part_keys[4], 1), M // 4, M).astype(jnp.int32),
        "block_live": place_ends((jax.random.randint(part_keys[5], (NL, NR), 0, 4) < 3).astype(jnp.int32), jax.random.fold_in(part_keys[5], 1), 0, 1),
    }


def build_mask(row_size, col_size, block_live):
    index = jnp.arange(M, dtype=jnp.int32)
    rows_ok = index[None, :] < row_size[:, None]
    cols_ok = index[None, :] < col_size[:, None]
    return (block_live[:, :, None, None] == 1) & rows_ok[:, None, :, None] & cols_ok[None, :, None, :]

def reference(two_site, left_env, right_env, row_size, col_size, block_live):
    live_mask = build_mask(row_size, col_size, block_live)
    start = jnp.where(live_mask, two_site, jnp.zeros_like(two_site))

    def apply(vector):

        def one_term(total, pair):
            left_block, right_block = pair
            left_part = jnp.einsum('aij,acjk->acik', left_block.astype(jnp.float32), vector.astype(jnp.float32)).astype(jnp.bfloat16)
            term_part = jnp.einsum('acij,cjk->acik', left_part.astype(jnp.float32), right_block.astype(jnp.float32)).astype(jnp.bfloat16)
            return (total + term_part.astype(jnp.float32), None)
        zeros = jnp.zeros(vector.shape, jnp.float32)
        total, _ = lax.scan(one_term, zeros, (left_env, right_env))
        return jnp.where(live_mask, total, jnp.zeros_like(total)).astype(jnp.bfloat16)
    first_image = apply(start)
    wide = first_image.astype(jnp.float32)
    norm_sum = jnp.sum(wide * wide)
    unit = (wide * lax.rsqrt(norm_sum / (NL * NR * M * M) + 1e-06)).astype(jnp.bfloat16)
    second_image = apply(unit)
    return (first_image, second_image)
```

```python
import functools

import jax
import jax.numpy as jnp
from jax import lax
from jax.experimental import pallas as pl
from jax.experimental.pallas import tpu as pltpu
from jax.sharding import PartitionSpec as P

AXES = ("blk", "term")


def move(value, pairs, terms):
    return lax.ppermute(
        value, AXES, [(a * terms + b, c * terms + d) for (a, b), (c, d) in pairs]
    )


def apply_tile(left, right, tile, keep):
    terms, width = left.shape[0], tile.shape[0]
    wide = jnp.dot(
        left[...].reshape(terms * width, width), tile, preferred_element_type=jnp.float32
    ).astype(jnp.bfloat16)
    total = jnp.zeros((width, width), jnp.float32)
    for t in range(terms):
        total += jnp.dot(
            wide[t * width : (t + 1) * width], right[t], preferred_element_type=jnp.float32
        )
    return jnp.where(keep, total, 0.0)


def keep_mask(width, rows, cols, live):
    at_row = lax.broadcasted_iota(jnp.int32, (width, width), 0)
    at_col = lax.broadcasted_iota(jnp.int32, (width, width), 1)
    return (at_row < rows) & (at_col < cols) & (live == 1)


def first_kernel(terms, own, place, rows, cols, live, tiles, *refs):
    lefts, rights = refs[:terms], refs[terms : terms + own * terms]
    image, left, right, partial = refs[terms + own * terms :]
    width = tiles.shape[-1]
    blk, term = place[0], place[1]
    for m in range(terms):
        left[term ^ m] = lefts[m][0, 0]
    for k in range(own * terms):
        right[blk ^ k] = rights[k][0, 0]
    partial[...] = jnp.zeros_like(partial)
    for o in range(own):
        col = term * own + o
        keep = keep_mask(width, rows[0], cols[col], live[0, col])
        start = jnp.where(keep, tiles[0, col], jnp.zeros((), tiles.dtype))
        out = apply_tile(left, right.at[pl.ds(o * terms, terms)], start, keep).astype(jnp.bfloat16)
        image[0, o] = out
        out = out.astype(jnp.float32)
        partial[...] += jnp.sum((out * out).reshape(-1, 8, width), axis=0)


def second_kernel(terms, own, place, rows, cols, live, image, left, right, raw):
    width = image.shape[-1]
    for o in range(own):
        col = place[1] * own + o
        keep = keep_mask(width, rows[0], cols[col], live[0, col])
        raw[0, o] = apply_tile(left, right.at[pl.ds(o * terms, terms)], image[0, o], keep)


def scale_kernel(count, raw, norm, image):
    total = jnp.sum(norm[...])
    image[...] = (raw[...] * lax.rsqrt(total / count + 1e-06)).astype(jnp.bfloat16)


def total_over(value, axis, size, other):
    step = 1
    while step < size:
        if axis == "blk":
            pairs = [((a, b), (a ^ step, b)) for a in range(size) for b in range(other)]
            value = value + move(value, pairs, other)
        else:
            pairs = [((a, b), (a, b ^ step)) for a in range(other) for b in range(size)]
            value = value + move(value, pairs, size)
        step *= 2
    return value


def local(blocks, terms, two_site, left_env, right_env, row_size, col_size, block_live):
    width = two_site.shape[2]
    n_cols = two_site.shape[1]
    own = n_cols // terms
    vmem, smem = pl.BlockSpec(memory_space=pltpu.VMEM), pl.BlockSpec(memory_space=pltpu.SMEM)
    params = pltpu.CompilerParams(vmem_limit_bytes=32 * 1024 * 1024)
    place = jnp.stack([lax.axis_index("blk"), lax.axis_index("term")]).astype(jnp.int32)

    rights = []
    for k in range(blocks):
        pairs = [
            ((c, t), (((c % own) * terms + t) ^ k, c // own))
            for c in range(blocks)
            for t in range(terms)
        ]
        rights.append(move(right_env, pairs, terms))
    lefts = [left_env] + [
        move(left_env, [((a, t), (a, t ^ m)) for a in range(blocks) for t in range(terms)], terms)
        for m in range(1, terms)
    ]

    first_image, left, right, partial = pl.pallas_call(
        functools.partial(first_kernel, terms, own),
        out_shape=(
            jax.ShapeDtypeStruct((1, own, width, width), jnp.bfloat16),
            jax.ShapeDtypeStruct((terms, width, width), jnp.bfloat16),
            jax.ShapeDtypeStruct((own * terms, width, width), jnp.bfloat16),
            jax.ShapeDtypeStruct((8, width), jnp.float32),
        ),
        in_specs=[smem] * 4 + [vmem] * (1 + terms + blocks),
        out_specs=(vmem,) * 4,
        compiler_params=params,
    )(place, row_size, col_size, block_live, two_site, *lefts, *rights)

    raw = pl.pallas_call(
        functools.partial(second_kernel, terms, own),
        out_shape=jax.ShapeDtypeStruct((1, own, width, width), jnp.float32),
        in_specs=[smem] * 4 + [vmem] * 3,
        out_specs=vmem,
        compiler_params=params,
    )(place, row_size, col_size, block_live, first_image, left, right)

    norm = total_over(total_over(partial, "term", terms, blocks), "blk", blocks, terms)
    second_image = pl.pallas_call(
        functools.partial(scale_kernel, float(blocks * n_cols * width * width)),
        out_shape=jax.ShapeDtypeStruct((1, own, width, width), jnp.bfloat16),
        in_specs=[vmem] * 2,
        out_specs=vmem,
        compiler_params=params,
    )(raw, norm)
    return first_image, second_image


def solution(mesh):
    return jax.shard_map(
        functools.partial(local, mesh.shape["blk"], mesh.shape["term"]),
        mesh=mesh,
        in_specs=(
            P(("runs", "blk"), None, None, None),
            P(("runs", "term"), "blk", None, None),
            P(("runs", "term"), "blk", None, None),
            P(("runs", "blk")),
            P("runs"),
            P(("runs", "blk"), None),
        ),
        out_specs=(P(("runs", "blk"), "term", None, None), P(("runs", "blk"), "term", None, None)),
        check_vma=False,
    )
```

```python
import functools

import jax
import jax.numpy as jnp
import numpy as np
from jax import lax
from jax.experimental import pallas as pl
from jax.experimental.pallas import tpu as pltpu
from jax.sharding import PartitionSpec as P

AXES = ("blk", "term")


def move(value, pairs, terms):
    return lax.ppermute(
        value, AXES, [(a * terms + b, c * terms + d) for (a, b), (c, d) in pairs]
    )


def right_routes(blocks, terms, own):
    half = blocks // 2
    steps, arrives = [], np.zeros((blocks, terms, blocks), np.int32)
    for k in range(blocks):
        pairs = []
        for c in range(blocks):
            for t in range(terms):
                i = (c % own) * terms + t
                a = ((i % 2) * half + i // 2) ^ k
                arrives[a, c // own, k] = i
                if (c, t) != (a, c // own):
                    pairs.append(((c, t), (a, c // own)))
        steps.append(pairs)
    return steps, arrives


def keep_mask(width, rows, cols, live):
    at_row = lax.broadcasted_iota(jnp.int32, (width, width), 0)
    at_col = lax.broadcasted_iota(jnp.int32, (width, width), 1)
    return (at_row < rows) & (at_col < cols) & (live == 1)


def dot(a, b):
    return jnp.dot(a, b, preferred_element_type=jnp.float32)


def left_kernel(terms, own, place, rows, cols, live, two_site, *refs):
    lefts, (products, tiles, sem) = refs[:terms], refs[terms:]
    blk, term = place[0], place[1]
    width = tiles.shape[-1]
    copy = pltpu.make_async_copy(two_site.at[0, pl.ds(term * own, own)], tiles, sem)
    copy.start()
    copy.wait()
    for o in range(own):
        col = term * own + o
        keep = keep_mask(width, rows[0], cols[col], live[0, col])
        start = jnp.where(keep, tiles[o], jnp.zeros((), tiles.dtype))
        for m in range(terms):
            products[o, term ^ m] = dot(lefts[m][0, 0], start).astype(jnp.bfloat16)


def right_sum(terms, own, place, arrives, products, mine, rights, total):
    total[...] = jnp.zeros_like(total)
    for k, right in enumerate(rights):
        o, t = arrives[k] // terms, arrives[k] % terms
        total[o] += dot(products[o, t], right[0, 0])

    @pl.when(place[0] // own == place[1])
    def _():
        o = place[0] % own
        total[o] += dot(products[o, place[1]], mine[0, 0])


def first_kernel(terms, own, place, arrives, rows, cols, live, products, mine, *refs):
    rights, (image, partial, total) = refs[:-3], refs[-3:]
    width = total.shape[-1]
    right_sum(terms, own, place, arrives, products, mine, rights, total)
    partial[...] = jnp.zeros_like(partial)
    for o in range(own):
        col = place[1] * own + o
        keep = keep_mask(width, rows[0], cols[col], live[0, col])
        out = jnp.where(keep, total[o], 0.0).astype(jnp.bfloat16)
        image[0, o] = out
        out = out.astype(jnp.float32)
        squares = jnp.sum((out * out).reshape(-1, 8, width), axis=0)
        for lane in range(0, width, 128):
            partial[...] += squares[:, lane : lane + 128]


def second_kernel(terms, own, place, arrives, rows, cols, live, image, mine, *refs):
    lefts, rights = refs[:terms], refs[terms:-4]
    final, raw, products, total = refs[-4:]
    width = total.shape[-1]
    final[...] = image[...]
    for o in range(own):
        for m in range(terms):
            products[o, place[1] ^ m] = dot(lefts[m][0, 0], image[0, o]).astype(jnp.bfloat16)
    right_sum(terms, own, place, arrives, products, mine, rights, total)
    for o in range(own):
        col = place[1] * own + o
        keep = keep_mask(width, rows[0], cols[col], live[0, col])
        raw[0, o] = jnp.where(keep, total[o], 0.0)


def scale_kernel(count, raw, norm, other, image):
    norm_sum = jnp.sum(norm[...] + other[...])
    image[...] = (raw[...] * lax.rsqrt(norm_sum / count + 1e-06)).astype(jnp.bfloat16)


def local(blocks, terms, two_site, left_env, right_env, row_size, col_size, block_live):
    width = two_site.shape[2]
    n_cols = two_site.shape[1]
    own = n_cols // terms
    vmem, smem = pl.BlockSpec(memory_space=pltpu.VMEM), pl.BlockSpec(memory_space=pltpu.SMEM)
    anywhere = pl.BlockSpec(memory_space=pl.ANY)
    params = pltpu.CompilerParams(vmem_limit_bytes=32 * 1024 * 1024)
    blk, term = lax.axis_index("blk"), lax.axis_index("term")
    place = jnp.stack([blk, term]).astype(jnp.int32)
    everyone = [(a, t) for a in range(blocks) for t in range(terms)]

    steps, table = right_routes(blocks, terms, own)
    arrives = jnp.asarray(table)[blk, term]
    rights = [move(right_env, pairs, terms) for pairs in steps]
    lefts = [left_env]
    for m in range(1, terms):
        if m % 2 == 0:
            lefts.append(move(left_env, [((a, t), (a, t ^ m)) for a, t in everyone], terms))
        else:
            lefts.append(move(lefts[m - 1], [((a, t), (a, t ^ 1)) for a, t in everyone], terms))

    tile = (own, width, width)
    dots = own * terms * 2 * width**3
    products = pl.pallas_call(
        functools.partial(left_kernel, terms, own),
        out_shape=jax.ShapeDtypeStruct((own, terms, width, width), jnp.bfloat16),
        in_specs=[smem] * 4 + [anywhere] + [vmem] * terms,
        out_specs=vmem,
        scratch_shapes=[pltpu.VMEM(tile, jnp.bfloat16), pltpu.SemaphoreType.DMA],
        compiler_params=params,
        cost_estimate=pl.CostEstimate(flops=dots, bytes_accessed=8 * width * width, transcendentals=0),
    )(place, row_size, col_size, block_live, two_site, *lefts)

    first, partial = pl.pallas_call(
        functools.partial(first_kernel, terms, own),
        out_shape=(
            jax.ShapeDtypeStruct((1,) + tile, jnp.bfloat16),
            jax.ShapeDtypeStruct((8, 128), jnp.float32),
        ),
        in_specs=[smem] * 5 + [vmem] * (2 + blocks),
        out_specs=(vmem,) * 2,
        scratch_shapes=[pltpu.VMEM(tile, jnp.float32)],
        compiler_params=params,
        cost_estimate=pl.CostEstimate(flops=dots, bytes_accessed=8 * width * width, transcendentals=0),
    )(place, arrives, row_size, col_size, block_live, products, right_env, *rights)

    first_image, raw = pl.pallas_call(
        functools.partial(second_kernel, terms, own),
        out_shape=(
            jax.ShapeDtypeStruct((1,) + tile, jnp.bfloat16),
            jax.ShapeDtypeStruct((1,) + tile, jnp.float32),
        ),
        in_specs=[smem] * 5 + [vmem] * (2 + terms + blocks),
        out_specs=(vmem,) * 2,
        scratch_shapes=[
            pltpu.VMEM((own, terms, width, width), jnp.bfloat16),
            pltpu.VMEM(tile, jnp.float32),
        ],
        compiler_params=params,
        cost_estimate=pl.CostEstimate(flops=2 * dots, bytes_accessed=8 * width * width, transcendentals=0),
    )(place, arrives, row_size, col_size, block_live, first, right_env, *lefts, *rights)

    other = jnp.zeros_like(partial)
    flips = [(0, 1 << s) for s in range((terms - 1).bit_length())]
    flips += [(1 << s, 0) for s in range((blocks - 1).bit_length())]
    norm = partial
    for da, dt in flips:
        norm = norm + other
        other = move(norm, [((a, t), (a ^ da, t ^ dt)) for a, t in everyone], terms)

    second_image = pl.pallas_call(
        functools.partial(scale_kernel, float(blocks * n_cols * width * width)),
        out_shape=jax.ShapeDtypeStruct((1,) + tile, jnp.bfloat16),
        in_specs=[vmem] * 3,
        out_specs=vmem,
        compiler_params=params,
    )(raw, norm, other)
    return first_image, second_image


def solution(mesh):
    return jax.shard_map(
        functools.partial(local, mesh.shape["blk"], mesh.shape["term"]),
        mesh=mesh,
        in_specs=(
            P(("runs", "blk"), None, None, None),
            P(("runs", "term"), "blk", None, None),
            P(("runs", "term"), "blk", None, None),
            P(("runs", "blk")),
            P("runs"),
            P(("runs", "blk"), None),
        ),
        out_specs=(P(("runs", "blk"), "term", None, None), P(("runs", "blk"), "term", None, None)),
        check_vma=False,
    )
```

```python
import functools

import jax
import jax.numpy as jnp
from jax import lax
from jax.experimental import pallas as pl
from jax.experimental.pallas import tpu as pltpu
from jax.sharding import PartitionSpec as P

AXES = ("blk", "term")


def move(value, pairs, terms):
    return lax.ppermute(
        value, AXES, [(a * terms + b, c * terms + d) for (a, b), (c, d) in pairs]
    )


def source_number(blocks, blk, step):
    half = blocks // 2
    place = blk ^ step
    return (place % half) * 2 + place // half


def right_routes(blocks, terms, own):
    steps = []
    for k in range(blocks):
        pairs = []
        for a in range(blocks):
            for group in range(terms):
                i = source_number(blocks, a, k)
                source = (group * own + i // terms, i % terms)
                if source != (a, group):
                    pairs.append((source, (a, group)))
        steps.append(pairs)
    return steps


def dot(a, b):
    return jnp.dot(a, b, preferred_element_type=jnp.float32)


def early_kernel(blocks, terms, own, two_site, rows, cols, live, *refs):
    rights, (start, keep, products, tiles, rows_at, cols_at, live_at, sems) = refs[:-8], refs[-8:]
    blk, term = lax.axis_index("blk"), lax.axis_index("term")
    width = tiles.shape[-1]
    copies = [
        pltpu.make_async_copy(two_site.at[0, pl.ds(term * own, own)], tiles, sems.at[0]),
        pltpu.make_async_copy(rows, rows_at, sems.at[1]),
        pltpu.make_async_copy(cols, cols_at, sems.at[2]),
        pltpu.make_async_copy(live, live_at, sems.at[3]),
    ]
    for copy in copies:
        copy.start()
    for copy in copies:
        copy.wait()
    at_row = lax.broadcasted_iota(jnp.int32, (width, width), 0)
    at_col = lax.broadcasted_iota(jnp.int32, (width, width), 1)
    for o in range(own):
        col = term * own + o
        mask = (at_row < rows_at[0]) & (at_col < cols_at[col]) & (live_at[0, col] == 1)
        start[o] = jnp.where(mask, tiles[o], jnp.zeros((), tiles.dtype))
        keep[o] = jnp.where(mask, 1.0, 0.0)
    for k, right in enumerate(rights):
        o = source_number(blocks, blk, k) // terms
        products[k] = dot(start[o], right[0, 0]).astype(jnp.bfloat16)


def finish(blocks, terms, own, tile, keep, mine, lefts, rights, early, products):
    blk, term = lax.axis_index("blk"), lax.axis_index("term")
    for k in range(blocks):
        i = source_number(blocks, blk, k)
        if k < blocks - len(rights):
            products[i] = early[k]
        else:
            right = rights[k - blocks + len(rights)]
            products[i] = dot(tile[i // terms], right[0, 0]).astype(jnp.bfloat16)

    @pl.when(blk // own == term)
    def _():
        o = blk % own
        products[o * terms + term] = dot(tile[o], mine[0, 0]).astype(jnp.bfloat16)

    sums = []
    for o in range(own):
        total = sum(dot(left[0, 0], products[o * terms + (term ^ m)]) for m, left in enumerate(lefts))
        sums.append(jnp.where(keep[o] != 0.0, total, 0.0))
    return sums


def first_kernel(blocks, terms, own, start, keep, early, mine, *refs):
    lefts, rights, (image, partial, products) = refs[:terms], refs[terms:-3], refs[-3:]
    width = start.shape[-1]
    squares = jnp.zeros((8, width), jnp.float32)
    for o, total in enumerate(finish(blocks, terms, own, start, keep, mine, lefts, rights, early, products)):
        out = total.astype(jnp.bfloat16)
        image[o] = out
        out = out.astype(jnp.float32)
        squares += jnp.sum((out * out).reshape(-1, 8, width), axis=0)
    partial[...] = sum(squares[:, lane : lane + 128] for lane in range(0, width, 128))


def second_kernel(blocks, terms, own, image, keep, mine, *refs):
    lefts, rights, (final, raw, products) = refs[:terms], refs[terms:-3], refs[-3:]
    final[0] = image[...]
    for o, total in enumerate(finish(blocks, terms, own, image, keep, mine, lefts, rights, None, products)):
        raw[0, o] = total


def scale_kernel(count, raw, norm, other, image):
    norm_sum = jnp.sum(norm[...] + other[...])
    image[...] = (raw[...] * lax.rsqrt(norm_sum / count + 1e-06)).astype(jnp.bfloat16)


def cost(dots, width):
    return pl.CostEstimate(flops=dots * 2 * width**3, bytes_accessed=8 * width**2, transcendentals=0)


def local(blocks, terms, two_site, left_env, right_env, row_size, col_size, block_live):
    width = two_site.shape[2]
    n_cols = two_site.shape[1]
    own = n_cols // terms
    vmem, hbm = pl.BlockSpec(memory_space=pltpu.VMEM), pl.BlockSpec(memory_space=pltpu.HBM)
    params = pltpu.CompilerParams(vmem_limit_bytes=32 * 1024 * 1024)
    everyone = [(a, t) for a in range(blocks) for t in range(terms)]

    rights = [move(right_env, pairs, terms) for pairs in right_routes(blocks, terms, own)]
    lefts = [left_env] + [None] * (terms - 1)
    for m in list(range(1, terms, 2)) + list(range(2, terms, 2)):
        source, hop = (left_env, m) if m % 2 else (lefts[m + 1], 1)
        lefts[m] = move(source, [((a, t), (a, t ^ hop)) for a, t in everyone], terms)

    tile = (own, width, width)
    early = blocks // 2
    start, keep, products = pl.pallas_call(
        functools.partial(early_kernel, blocks, terms, own),
        out_shape=(
            jax.ShapeDtypeStruct(tile, jnp.bfloat16),
            jax.ShapeDtypeStruct(tile, jnp.float32),
            jax.ShapeDtypeStruct((early, width, width), jnp.bfloat16),
        ),
        in_specs=[hbm] * 4 + [vmem] * early,
        out_specs=(vmem,) * 3,
        scratch_shapes=[
            pltpu.VMEM(tile, jnp.bfloat16),
            pltpu.SMEM(row_size.shape, jnp.int32),
            pltpu.SMEM(col_size.shape, jnp.int32),
            pltpu.SMEM(block_live.shape, jnp.int32),
            pltpu.SemaphoreType.DMA((4,)),
        ],
        compiler_params=params,
        cost_estimate=cost(early, width),
    )(two_site, row_size, col_size, block_live, *rights[:early])

    work = [pltpu.VMEM((blocks, width, width), jnp.bfloat16)]
    first, partial = pl.pallas_call(
        functools.partial(first_kernel, blocks, terms, own),
        out_shape=(
            jax.ShapeDtypeStruct(tile, jnp.bfloat16),
            jax.ShapeDtypeStruct((8, 128), jnp.float32),
        ),
        in_specs=[vmem] * (4 + terms + blocks - early),
        out_specs=(vmem,) * 2,
        scratch_shapes=work,
        compiler_params=params,
        cost_estimate=cost(2 * blocks - early, width),
    )(start, keep, products, right_env, *lefts, *rights[early:])

    first_image, raw = pl.pallas_call(
        functools.partial(second_kernel, blocks, terms, own),
        out_shape=(
            jax.ShapeDtypeStruct((1,) + tile, jnp.bfloat16),
            jax.ShapeDtypeStruct((1,) + tile, jnp.float32),
        ),
        in_specs=[vmem] * (3 + terms + blocks),
        out_specs=(vmem,) * 2,
        scratch_shapes=work,
        compiler_params=params,
        cost_estimate=cost(2 * blocks, width),
    )(first, keep, right_env, *lefts, *rights)

    flips = [(0, 1)] + [(0, 1 | 1 << s) for s in range(1, (terms - 1).bit_length())]
    flips += [(1 << s, 1) for s in range((blocks - 1).bit_length())]
    norm, other = partial, None
    for da, dt in flips:
        norm = norm if other is None else norm + other
        other = move(norm, [((a, t), (a ^ da, t ^ dt)) for a, t in everyone], terms)

    second_image = pl.pallas_call(
        functools.partial(scale_kernel, float(blocks * n_cols * width * width)),
        out_shape=jax.ShapeDtypeStruct((1,) + tile, jnp.bfloat16),
        in_specs=[vmem] * 3,
        out_specs=vmem,
        compiler_params=params,
    )(raw, norm, other)
    return first_image, second_image


def solution(mesh):
    return jax.shard_map(
        functools.partial(local, mesh.shape["blk"], mesh.shape["term"]),
        mesh=mesh,
        in_specs=(
            P(("runs", "blk"), None, None, None),
            P(("runs", "term"), "blk", None, None),
            P(("runs", "term"), "blk", None, None),
            P(("runs", "blk")),
            P("runs"),
            P(("runs", "blk"), None),
        ),
        out_specs=(P(("runs", "blk"), "term", None, None), P(("runs", "blk"), "term", None, None)),
        check_vma=False,
    )
```

```python
import functools

import jax
import jax.numpy as jnp
from jax import lax
from jax.experimental import pallas as pl
from jax.experimental.pallas import tpu as pltpu
from jax.sharding import PartitionSpec as P

AXES = ("blk", "term")


def move(value, pairs, terms):
    return lax.ppermute(
        value, AXES, [(a * terms + b, c * terms + d) for (a, b), (c, d) in pairs]
    )


ORDERS = ((2, 0, 1, 3), (1, 3, 0, 2), (1, 3, 0, 2), (0, 2, 3, 1))


def source_number(blocks, own, blk, term, step):
    place = blk ^ step
    if blocks == 4 and own == 1:
        packed = sum(i << (8 * g + 2 * p) for g, order in enumerate(ORDERS) for i, p in enumerate(order))
        if not isinstance(place, int):
            packed = jnp.int32(packed - (packed >> 31 << 32))
        return (packed >> (8 * term + 2 * place)) & 3
    half = blocks // 2
    return (place % half) * 2 + place // half


def right_routes(blocks, terms, own):
    steps = []
    for k in range(blocks):
        pairs = []
        for a in range(blocks):
            for group in range(terms):
                i = source_number(blocks, own, a, group, k)
                source = (group * own + i // terms, i % terms)
                if source != (a, group):
                    pairs.append((source, (a, group)))
        steps.append(pairs)
    return steps


def dot(a, b):
    return jnp.dot(a, b, preferred_element_type=jnp.float32)


def early_kernel(blocks, terms, own, two_site, rows, cols, live, *refs):
    rights, (start, keep, products, tiles, rows_at, cols_at, live_at, sems) = refs[:-8], refs[-8:]
    blk, term = lax.axis_index("blk"), lax.axis_index("term")
    width = tiles.shape[-1]
    copies = [
        pltpu.make_async_copy(two_site.at[0, pl.ds(term * own, own)], tiles, sems.at[0]),
        pltpu.make_async_copy(rows, rows_at, sems.at[1]),
        pltpu.make_async_copy(cols, cols_at, sems.at[2]),
        pltpu.make_async_copy(live, live_at, sems.at[3]),
    ]
    for copy in copies:
        copy.start()
    for copy in copies:
        copy.wait()
    at_row = lax.broadcasted_iota(jnp.int32, (width, width), 0)
    at_col = lax.broadcasted_iota(jnp.int32, (width, width), 1)
    for o in range(own):
        col = term * own + o
        mask = (at_row < rows_at[0]) & (at_col < cols_at[col]) & (live_at[0, col] == 1)
        start[o] = jnp.where(mask, tiles[o], jnp.zeros((), tiles.dtype))
        keep[o] = jnp.where(mask, 1.0, 0.0)
    for k, right in enumerate(rights):
        o = source_number(blocks, own, blk, term, k) // terms
        products[k] = dot(start[o], right[0, 0]).astype(jnp.bfloat16)


def finish(blocks, terms, own, tile, keep, mine, lefts, rights, early, products):
    blk, term = lax.axis_index("blk"), lax.axis_index("term")
    for k in range(blocks):
        i = source_number(blocks, own, blk, term, k)
        if k < blocks - len(rights):
            products[i] = early[k]
        else:
            right = rights[k - blocks + len(rights)]
            products[i] = dot(tile[i // terms], right[0, 0]).astype(jnp.bfloat16)

    @pl.when(blk // own == term)
    def _():
        o = blk % own
        products[o * terms + term] = dot(tile[o], mine[0, 0]).astype(jnp.bfloat16)

    sums = []
    for o in range(own):
        total = sum(dot(left[0, 0], products[o * terms + (term ^ m)]) for m, left in enumerate(lefts))
        sums.append(jnp.where(keep[o] != 0.0, total, 0.0))
    return sums


def first_kernel(blocks, terms, own, start, keep, early, mine, *refs):
    lefts, rights, (image, partial, products) = refs[:terms], refs[terms:-3], refs[-3:]
    width = start.shape[-1]
    squares = jnp.zeros((8, width), jnp.float32)
    for o, total in enumerate(finish(blocks, terms, own, start, keep, mine, lefts, rights, early, products)):
        out = total.astype(jnp.bfloat16)
        image[o] = out
        out = out.astype(jnp.float32)
        squares += jnp.sum((out * out).reshape(-1, 8, width), axis=0)
    partial[...] = sum(squares[:, lane : lane + 128] for lane in range(0, width, 128))


def second_kernel(blocks, terms, own, image, keep, mine, *refs):
    lefts, rights, (final, raw, products) = refs[:terms], refs[terms:-3], refs[-3:]
    final[0] = image[...]
    for o, total in enumerate(finish(blocks, terms, own, image, keep, mine, lefts, rights, None, products)):
        raw[0, o] = total


def scale_kernel(count, raw, norm, other, image):
    norm_sum = jnp.sum(norm[...] + other[...])
    image[...] = (raw[...] * lax.rsqrt(norm_sum / count + 1e-06)).astype(jnp.bfloat16)


def cost(dots, width):
    return pl.CostEstimate(flops=dots * 2 * width**3, bytes_accessed=8 * width**2, transcendentals=0)


def local(blocks, terms, two_site, left_env, right_env, row_size, col_size, block_live):
    width = two_site.shape[2]
    n_cols = two_site.shape[1]
    own = n_cols // terms
    vmem, hbm = pl.BlockSpec(memory_space=pltpu.VMEM), pl.BlockSpec(memory_space=pltpu.HBM)
    params = pltpu.CompilerParams(vmem_limit_bytes=32 * 1024 * 1024)
    everyone = [(a, t) for a in range(blocks) for t in range(terms)]

    rights = [move(right_env, pairs, terms) for pairs in right_routes(blocks, terms, own)]
    lefts = [left_env] + [None] * (terms - 1)
    for m in list(range(1, terms, 2)) + list(range(2, terms, 2)):
        source, hop = (left_env, m) if m % 2 else (lefts[m + 1], 1)
        lefts[m] = move(source, [((a, t), (a, t ^ hop)) for a, t in everyone], terms)

    tile = (own, width, width)
    early = blocks // 2
    start, keep, products = pl.pallas_call(
        functools.partial(early_kernel, blocks, terms, own),
        out_shape=(
            jax.ShapeDtypeStruct(tile, jnp.bfloat16),
            jax.ShapeDtypeStruct(tile, jnp.float32),
            jax.ShapeDtypeStruct((early, width, width), jnp.bfloat16),
        ),
        in_specs=[hbm] * 4 + [vmem] * early,
        out_specs=(vmem,) * 3,
        scratch_shapes=[
            pltpu.VMEM(tile, jnp.bfloat16),
            pltpu.SMEM(row_size.shape, jnp.int32),
            pltpu.SMEM(col_size.shape, jnp.int32),
            pltpu.SMEM(block_live.shape, jnp.int32),
            pltpu.SemaphoreType.DMA((4,)),
        ],
        compiler_params=params,
        cost_estimate=cost(early, width),
    )(two_site, row_size, col_size, block_live, *rights[:early])

    work = [pltpu.VMEM((blocks, width, width), jnp.bfloat16)]
    first, partial = pl.pallas_call(
        functools.partial(first_kernel, blocks, terms, own),
        out_shape=(
            jax.ShapeDtypeStruct(tile, jnp.bfloat16),
            jax.ShapeDtypeStruct((8, 128), jnp.float32),
        ),
        in_specs=[vmem] * (4 + terms + blocks - early),
        out_specs=(vmem,) * 2,
        scratch_shapes=work,
        compiler_params=params,
        cost_estimate=cost(2 * blocks - early, width),
    )(start, keep, products, right_env, *lefts, *rights[early:])

    first_image, raw = pl.pallas_call(
        functools.partial(second_kernel, blocks, terms, own),
        out_shape=(
            jax.ShapeDtypeStruct((1,) + tile, jnp.bfloat16),
            jax.ShapeDtypeStruct((1,) + tile, jnp.float32),
        ),
        in_specs=[vmem] * (3 + terms + blocks),
        out_specs=(vmem,) * 2,
        scratch_shapes=work,
        compiler_params=params,
        cost_estimate=cost(2 * blocks, width),
    )(first, keep, right_env, *lefts, *rights)

    flips = [(0, 1)] + [(0, 1 | 1 << s) for s in range(1, (terms - 1).bit_length())]
    flips += [(1 << s, 1) for s in range((blocks - 1).bit_length())]
    norm, other = partial, None
    for da, dt in flips:
        norm = norm if other is None else norm + other
        other = move(norm, [((a, t), (a ^ da, t ^ dt)) for a, t in everyone], terms)

    second_image = pl.pallas_call(
        functools.partial(scale_kernel, float(blocks * n_cols * width * width)),
        out_shape=jax.ShapeDtypeStruct((1,) + tile, jnp.bfloat16),
        in_specs=[vmem] * 3,
        out_specs=vmem,
        compiler_params=params,
    )(raw, norm, other)
    return first_image, second_image


def solution(mesh):
    return jax.shard_map(
        functools.partial(local, mesh.shape["blk"], mesh.shape["term"]),
        mesh=mesh,
        in_specs=(
            P(("runs", "blk"), None, None, None),
            P(("runs", "term"), "blk", None, None),
            P(("runs", "term"), "blk", None, None),
            P(("runs", "blk")),
            P("runs"),
            P(("runs", "blk"), None),
        ),
        out_specs=(P(("runs", "blk"), "term", None, None), P(("runs", "blk"), "term", None, None)),
        check_vma=False,
    )
```

```python
import functools

import jax
import jax.numpy as jnp
from jax import lax
from jax.experimental import pallas as pl
from jax.experimental.pallas import tpu as pltpu
from jax.sharding import PartitionSpec as P

AXES = ("blk", "term")


def move(value, pairs, terms):
    return lax.ppermute(
        value, AXES, [(a * terms + b, c * terms + d) for (a, b), (c, d) in pairs]
    )


ORDERS = ((2, 0, 1, 3), (1, 3, 0, 2), (1, 3, 0, 2), (0, 2, 3, 1))
STEPS = (2, 3, 1, 0)


def steps_of(blocks, own):
    return STEPS if blocks == 4 and own == 1 else range(blocks)


def source_number(blocks, own, blk, term, step):
    place = blk ^ step
    if blocks == 4 and own == 1:
        packed = sum(i << (8 * g + 2 * p) for g, order in enumerate(ORDERS) for i, p in enumerate(order))
        if not isinstance(place, int):
            packed = jnp.int32(packed - (packed >> 31 << 32))
        return (packed >> (8 * term + 2 * place)) & 3
    half = blocks // 2
    return (place % half) * 2 + place // half


def right_routes(blocks, terms, own):
    routes = []
    for step in steps_of(blocks, own):
        pairs = []
        for a in range(blocks):
            for group in range(terms):
                i = source_number(blocks, own, a, group, step)
                source = (group * own + i // terms, i % terms)
                if source != (a, group):
                    pairs.append((source, (a, group)))
        routes.append(pairs)
    return routes


def dot(a, b):
    return jnp.dot(a, b, preferred_element_type=jnp.float32)


def start_kernel(own, two_site, rows, cols, live, start, keep, tiles, rows_at, cols_at, live_at, sems):
    term = lax.axis_index("term")
    width = tiles.shape[-1]
    copies = [
        pltpu.make_async_copy(two_site.at[0, pl.ds(term * own, own)], tiles, sems.at[0]),
        pltpu.make_async_copy(rows, rows_at, sems.at[1]),
        pltpu.make_async_copy(cols, cols_at, sems.at[2]),
        pltpu.make_async_copy(live, live_at, sems.at[3]),
    ]
    for copy in copies:
        copy.start()
    for copy in copies:
        copy.wait()
    at_row = lax.broadcasted_iota(jnp.int32, (width, width), 0)
    at_col = lax.broadcasted_iota(jnp.int32, (width, width), 1)
    for o in range(own):
        col = term * own + o
        mask = (at_row < rows_at[0]) & (at_col < cols_at[col]) & (live_at[0, col] == 1)
        start[o] = jnp.where(mask, tiles[o], jnp.zeros((), tiles.dtype))
        keep[o] = jnp.where(mask, 1.0, 0.0)


def apply_tiles(blocks, terms, own, tile, keep, mine, lefts, rights, products):
    blk, term = lax.axis_index("blk"), lax.axis_index("term")
    for step, right in zip(steps_of(blocks, own), rights):
        i = source_number(blocks, own, blk, term, step)
        products[i] = dot(tile[i // terms], right[0, 0]).astype(jnp.bfloat16)

    @pl.when(blk // own == term)
    def _():
        o = blk % own
        products[o * terms + term] = dot(tile[o], mine[0, 0]).astype(jnp.bfloat16)

    sums = []
    for o in range(own):
        total = sum(dot(left[0, 0], products[o * terms + (term ^ m)]) for m, left in enumerate(lefts))
        sums.append(jnp.where(keep[o] != 0.0, total, 0.0))
    return sums


def first_kernel(blocks, terms, own, start, keep, mine, *refs):
    lefts, rights, (image, partial, products) = refs[:terms], refs[terms:-3], refs[-3:]
    width = start.shape[-1]
    squares = jnp.zeros((8, width), jnp.float32)
    for o, total in enumerate(apply_tiles(blocks, terms, own, start, keep, mine, lefts, rights, products)):
        out = total.astype(jnp.bfloat16)
        image[o] = out
        out = out.astype(jnp.float32)
        squares += jnp.sum((out * out).reshape(-1, 8, width), axis=0)
    partial[...] = sum(squares[:, lane : lane + 128] for lane in range(0, width, 128))


def second_kernel(blocks, terms, own, image, keep, mine, *refs):
    lefts, rights, (final, raw, products) = refs[:terms], refs[terms:-3], refs[-3:]
    final[0] = image[...]
    for o, total in enumerate(apply_tiles(blocks, terms, own, image, keep, mine, lefts, rights, products)):
        raw[0, o] = total


def scale_kernel(count, raw, norm, other, image):
    norm_sum = jnp.sum(norm[...] + other[...])
    image[...] = (raw[...] * lax.rsqrt(norm_sum / count + 1e-06)).astype(jnp.bfloat16)


def cost(dots, width):
    return pl.CostEstimate(flops=dots * 2 * width**3, bytes_accessed=8 * width**2, transcendentals=0)


def local(blocks, terms, two_site, left_env, right_env, row_size, col_size, block_live):
    width = two_site.shape[2]
    n_cols = two_site.shape[1]
    own = n_cols // terms
    vmem, hbm = pl.BlockSpec(memory_space=pltpu.VMEM), pl.BlockSpec(memory_space=pltpu.HBM)
    params = pltpu.CompilerParams(vmem_limit_bytes=32 * 1024 * 1024)
    everyone = [(a, t) for a in range(blocks) for t in range(terms)]

    rights = [move(right_env, pairs, terms) for pairs in right_routes(blocks, terms, own)]
    lefts = [left_env] + [None] * (terms - 1)
    for m in list(range(1, terms, 2)) + list(range(2, terms, 2)):
        source, hop = (left_env, m) if m % 2 else (lefts[m + 1], 1)
        lefts[m] = move(source, [((a, t), (a, t ^ hop)) for a, t in everyone], terms)

    tile = (own, width, width)
    start, keep = pl.pallas_call(
        functools.partial(start_kernel, own),
        out_shape=(
            jax.ShapeDtypeStruct(tile, jnp.bfloat16),
            jax.ShapeDtypeStruct(tile, jnp.float32),
        ),
        in_specs=[hbm] * 4,
        out_specs=(vmem,) * 2,
        scratch_shapes=[
            pltpu.VMEM(tile, jnp.bfloat16),
            pltpu.SMEM(row_size.shape, jnp.int32),
            pltpu.SMEM(col_size.shape, jnp.int32),
            pltpu.SMEM(block_live.shape, jnp.int32),
            pltpu.SemaphoreType.DMA((4,)),
        ],
        compiler_params=params,
        cost_estimate=cost(0, width),
    )(two_site, row_size, col_size, block_live)

    def apply_call(kernel, operand, outs):
        return pl.pallas_call(
            functools.partial(kernel, blocks, terms, own),
            out_shape=outs,
            in_specs=[vmem] * (3 + terms + blocks),
            out_specs=(vmem,) * 2,
            scratch_shapes=[pltpu.VMEM((blocks, width, width), jnp.bfloat16)],
            compiler_params=params,
            cost_estimate=cost(2 * blocks, width),
        )(operand, keep, right_env, *lefts, *rights)

    first, partial = apply_call(
        first_kernel,
        start,
        (jax.ShapeDtypeStruct(tile, jnp.bfloat16), jax.ShapeDtypeStruct((8, 128), jnp.float32)),
    )
    first_image, raw = apply_call(
        second_kernel,
        first,
        (jax.ShapeDtypeStruct((1,) + tile, jnp.bfloat16), jax.ShapeDtypeStruct((1,) + tile, jnp.float32)),
    )

    flips = [(0, 1)] + [(0, 1 | 1 << s) for s in range(1, (terms - 1).bit_length())]
    flips += [(1 << s, 1) for s in range((blocks - 1).bit_length())]
    norm, other = partial, None
    for da, dt in flips:
        norm = norm if other is None else norm + other
        other = move(norm, [((a, t), (a ^ da, t ^ dt)) for a, t in everyone], terms)

    second_image = pl.pallas_call(
        functools.partial(scale_kernel, float(blocks * n_cols * width * width)),
        out_shape=jax.ShapeDtypeStruct((1,) + tile, jnp.bfloat16),
        in_specs=[vmem] * 3,
        out_specs=vmem,
        compiler_params=params,
    )(raw, norm, other)
    return first_image, second_image


def solution(mesh):
    return jax.shard_map(
        functools.partial(local, mesh.shape["blk"], mesh.shape["term"]),
        mesh=mesh,
        in_specs=(
            P(("runs", "blk"), None, None, None),
            P(("runs", "term"), "blk", None, None),
            P(("runs", "term"), "blk", None, None),
            P(("runs", "blk")),
            P("runs"),
            P(("runs", "blk"), None),
        ),
        out_specs=(P(("runs", "blk"), "term", None, None), P(("runs", "blk"), "term", None, None)),
        check_vma=False,
    )
```

```python
import functools

import jax
import jax.numpy as jnp
from jax import lax
from jax.experimental import pallas as pl
from jax.experimental.pallas import tpu as pltpu
from jax.sharding import PartitionSpec as P

AXES = ("blk", "term")


def move(value, pairs, terms):
    return lax.ppermute(
        value, AXES, [(a * terms + b, c * terms + d) for (a, b), (c, d) in pairs]
    )


ORDERS = ((2, 0, 1, 3), (1, 3, 0, 2), (1, 3, 0, 2), (0, 2, 3, 1))
STEPS = (2, 3, 1, 0)


def steps_of(blocks, own):
    return STEPS if blocks == 4 and own == 1 else range(blocks)


def source_number(blocks, own, blk, term, step):
    place = blk ^ step
    if blocks == 4 and own == 1:
        packed = sum(i << (8 * g + 2 * p) for g, order in enumerate(ORDERS) for i, p in enumerate(order))
        if not isinstance(place, int):
            packed = jnp.int32(packed - (packed >> 31 << 32))
        return (packed >> (8 * term + 2 * place)) & 3
    half = blocks // 2
    return (place % half) * 2 + place // half


def right_routes(blocks, terms, own):
    routes = []
    for step in steps_of(blocks, own):
        pairs = []
        for a in range(blocks):
            for group in range(terms):
                i = source_number(blocks, own, a, group, step)
                source = (group * own + i // terms, i % terms)
                if source != (a, group):
                    pairs.append((source, (a, group)))
        routes.append(pairs)
    return routes


def dot(a, b):
    return jnp.dot(a, b, preferred_element_type=jnp.float32)


def start_kernel(own, two_site, rows, cols, live, start, keep, tiles, rows_at, cols_at, live_at, sems):
    term = lax.axis_index("term")
    width = tiles.shape[-1]
    copies = [
        pltpu.make_async_copy(two_site.at[0, pl.ds(term * own, own)], tiles, sems.at[0]),
        pltpu.make_async_copy(rows, rows_at, sems.at[1]),
        pltpu.make_async_copy(cols, cols_at, sems.at[2]),
        pltpu.make_async_copy(live, live_at, sems.at[3]),
    ]
    for copy in copies:
        copy.start()
    for copy in copies:
        copy.wait()
    at_row = lax.broadcasted_iota(jnp.int32, (width, width), 0)
    at_col = lax.broadcasted_iota(jnp.int32, (width, width), 1)
    for o in range(own):
        col = term * own + o
        mask = (at_row < rows_at[0]) & (at_col < cols_at[col]) & (live_at[0, col] == 1)
        start[o] = jnp.where(mask, tiles[o], jnp.zeros((), tiles.dtype))
        keep[o] = jnp.where(mask, 1.0, 0.0)


def apply_tiles(blocks, terms, own, tile, keep, mine, lefts, rights, products):
    blk, term = lax.axis_index("blk"), lax.axis_index("term")
    for step, right in zip(steps_of(blocks, own), rights):
        i = source_number(blocks, own, blk, term, step)
        products[i] = dot(tile[i // terms], right[0, 0]).astype(jnp.bfloat16)

    @pl.when(blk // own == term)
    def _():
        o = blk % own
        products[o * terms + term] = dot(tile[o], mine[0, 0]).astype(jnp.bfloat16)

    sums = []
    for o in range(own):
        total = sum(dot(left[0, 0], products[o * terms + (term ^ m)]) for m, left in enumerate(lefts))
        sums.append(jnp.where(keep[o] != 0.0, total, 0.0))
    return sums


def first_kernel(blocks, terms, own, start, keep, mine, *refs):
    lefts, rights, (image, partial, products) = refs[:terms], refs[terms:-3], refs[-3:]
    width = start.shape[-1]
    squares = jnp.zeros((8, width), jnp.float32)
    for o, total in enumerate(apply_tiles(blocks, terms, own, start, keep, mine, lefts, rights, products)):
        out = total.astype(jnp.bfloat16)
        image[o] = out
        out = out.astype(jnp.float32)
        squares += jnp.sum((out * out).reshape(-1, 8, width), axis=0)
    partial[...] = sum(squares[:, lane : lane + 128] for lane in range(0, width, 128))


def second_kernel(blocks, terms, own, image, keep, mine, *refs):
    lefts, rights, (final, raw, products) = refs[:terms], refs[terms:-3], refs[-3:]
    final[0] = image[...]
    for o, total in enumerate(apply_tiles(blocks, terms, own, image, keep, mine, lefts, rights, products)):
        raw[0, o] = total


def scale_kernel(count, raw, norm, other, image):
    norm_sum = jnp.sum(norm[...] + other[...])
    image[...] = (raw[...] * lax.rsqrt(norm_sum / count + 1e-06)).astype(jnp.bfloat16)


def cost(dots, width):
    return pl.CostEstimate(flops=dots * 2 * width**3, bytes_accessed=8 * width**2, transcendentals=0)


def local(blocks, terms, two_site, left_env, right_env, row_size, col_size, block_live):
    width = two_site.shape[2]
    n_cols = two_site.shape[1]
    own = n_cols // terms
    vmem, hbm = pl.BlockSpec(memory_space=pltpu.VMEM), pl.BlockSpec(memory_space=pltpu.HBM)
    params = pltpu.CompilerParams(vmem_limit_bytes=32 * 1024 * 1024)
    everyone = [(a, t) for a in range(blocks) for t in range(terms)]

    rights = [move(right_env, pairs, terms) for pairs in right_routes(blocks, terms, own)]
    lefts = [left_env] + [None] * (terms - 1)
    for m in list(range(3, terms, 2)) + list(range(2, terms, 2)) + [1]:
        source, hop = (left_env, m) if m % 2 else (lefts[m + 1], 1)
        if m == 1:
            source, _ = lax.optimization_barrier((left_env, rights[-1]))
        lefts[m] = move(source, [((a, t), (a, t ^ hop)) for a, t in everyone], terms)

    tile = (own, width, width)
    start, keep = pl.pallas_call(
        functools.partial(start_kernel, own),
        out_shape=(
            jax.ShapeDtypeStruct(tile, jnp.bfloat16),
            jax.ShapeDtypeStruct(tile, jnp.float32),
        ),
        in_specs=[hbm] * 4,
        out_specs=(vmem,) * 2,
        scratch_shapes=[
            pltpu.VMEM(tile, jnp.bfloat16),
            pltpu.SMEM(row_size.shape, jnp.int32),
            pltpu.SMEM(col_size.shape, jnp.int32),
            pltpu.SMEM(block_live.shape, jnp.int32),
            pltpu.SemaphoreType.DMA((4,)),
        ],
        compiler_params=params,
        cost_estimate=cost(0, width),
    )(two_site, row_size, col_size, block_live)

    def apply_call(kernel, operand, outs):
        return pl.pallas_call(
            functools.partial(kernel, blocks, terms, own),
            out_shape=outs,
            in_specs=[vmem] * (3 + terms + blocks),
            out_specs=(vmem,) * 2,
            scratch_shapes=[pltpu.VMEM((blocks, width, width), jnp.bfloat16)],
            compiler_params=params,
            cost_estimate=cost(2 * blocks, width),
        )(operand, keep, right_env, *lefts, *rights)

    first, partial = apply_call(
        first_kernel,
        start,
        (jax.ShapeDtypeStruct(tile, jnp.bfloat16), jax.ShapeDtypeStruct((8, 128), jnp.float32)),
    )
    first_image, raw = apply_call(
        second_kernel,
        first,
        (jax.ShapeDtypeStruct((1,) + tile, jnp.bfloat16), jax.ShapeDtypeStruct((1,) + tile, jnp.float32)),
    )

    flips = [(0, 1)] + [(0, 1 | 1 << s) for s in range(1, (terms - 1).bit_length())]
    flips += [(1 << s, 1) for s in range((blocks - 1).bit_length())]
    norm, other = partial, None
    for da, dt in flips:
        norm = norm if other is None else norm + other
        other = move(norm, [((a, t), (a ^ da, t ^ dt)) for a, t in everyone], terms)

    second_image = pl.pallas_call(
        functools.partial(scale_kernel, float(blocks * n_cols * width * width)),
        out_shape=jax.ShapeDtypeStruct((1,) + tile, jnp.bfloat16),
        in_specs=[vmem] * 3,
        out_specs=vmem,
        compiler_params=params,
    )(raw, norm, other)
    return first_image, second_image


def solution(mesh):
    return jax.shard_map(
        functools.partial(local, mesh.shape["blk"], mesh.shape["term"]),
        mesh=mesh,
        in_specs=(
            P(("runs", "blk"), None, None, None),
            P(("runs", "term"), "blk", None, None),
            P(("runs", "term"), "blk", None, None),
            P(("runs", "blk")),
            P("runs"),
            P(("runs", "blk"), None),
        ),
        out_specs=(P(("runs", "blk"), "term", None, None), P(("runs", "blk"), "term", None, None)),
        check_vma=False,
    )
```

```python
import functools

import jax
import jax.numpy as jnp
from jax import lax
from jax.experimental import pallas as pl
from jax.experimental.pallas import tpu as pltpu
from jax.sharding import PartitionSpec as P

AXES = ("blk", "term")


def move(value, pairs, terms):
    return lax.ppermute(
        value, AXES, [(a * terms + b, c * terms + d) for (a, b), (c, d) in pairs]
    )


ROUTES = (
    ((0, 2, 3, 1), (3, 1, 0, 2), (1, 3, 2, 0), (2, 0, 1, 3)),
    ((3, 1, 2, 0), (1, 3, 0, 2), (2, 0, 3, 1), (0, 2, 1, 3)),
    ((3, 1, 2, 0), (1, 3, 0, 2), (0, 2, 1, 3), (2, 0, 3, 1)),
    ((0, 2, 1, 3), (2, 0, 3, 1), (1, 3, 0, 2), (3, 1, 2, 0)),
)


def source_number(blocks, own, blk, term, step):
    if blocks == 4 and own == 1:
        packed = sum(i << (8 * g + 2 * p) for g, r in enumerate(ROUTES) for i, p in enumerate(r[step]))
        if not isinstance(blk, int):
            packed = jnp.int32(packed - (packed >> 31 << 32))
        return (packed >> (8 * term + 2 * blk)) & 3
    half, place = blocks // 2, blk ^ step
    return (place % half) * 2 + place // half


def right_routes(blocks, terms, own):
    routes = []
    for step in range(blocks):
        pairs = []
        for a in range(blocks):
            for group in range(terms):
                i = source_number(blocks, own, a, group, step)
                source = (group * own + i // terms, i % terms)
                if source != (a, group):
                    pairs.append((source, (a, group)))
        routes.append(pairs)
    return routes


def dot(a, b):
    return jnp.dot(a, b, preferred_element_type=jnp.float32)


def start_kernel(own, two_site, rows, cols, live, start, keep, tiles, rows_at, cols_at, live_at, sems):
    term = lax.axis_index("term")
    width = tiles.shape[-1]
    copies = [
        pltpu.make_async_copy(two_site.at[0, pl.ds(term * own, own)], tiles, sems.at[0]),
        pltpu.make_async_copy(rows, rows_at, sems.at[1]),
        pltpu.make_async_copy(cols, cols_at, sems.at[2]),
        pltpu.make_async_copy(live, live_at, sems.at[3]),
    ]
    for copy in copies:
        copy.start()
    for copy in copies:
        copy.wait()
    at_row = lax.broadcasted_iota(jnp.int32, (width, width), 0)
    at_col = lax.broadcasted_iota(jnp.int32, (width, width), 1)
    for o in range(own):
        col = term * own + o
        mask = (at_row < rows_at[0]) & (at_col < cols_at[col]) & (live_at[0, col] == 1)
        start[o] = jnp.where(mask, tiles[o], jnp.zeros((), tiles.dtype))
        keep[o] = jnp.where(mask, 1.0, 0.0)


def apply_tiles(blocks, terms, own, tile, keep, mine, lefts, rights, products):
    blk, term = lax.axis_index("blk"), lax.axis_index("term")
    for step, right in enumerate(rights):
        i = source_number(blocks, own, blk, term, step)
        products[i] = dot(tile[i // terms], right[0, 0]).astype(jnp.bfloat16)

    @pl.when(blk // own == term)
    def _():
        o = blk % own
        products[o * terms + term] = dot(tile[o], mine[0, 0]).astype(jnp.bfloat16)

    sums = []
    for o in range(own):
        total = sum(dot(left[0, 0], products[o * terms + (term ^ m)]) for m, left in enumerate(lefts))
        sums.append(jnp.where(keep[o] != 0.0, total, 0.0))
    return sums


def first_kernel(blocks, terms, own, start, keep, mine, *refs):
    lefts, rights, (image, partial, products) = refs[:terms], refs[terms:-3], refs[-3:]
    width = start.shape[-1]
    squares = jnp.zeros((8, width), jnp.float32)
    for o, total in enumerate(apply_tiles(blocks, terms, own, start, keep, mine, lefts, rights, products)):
        out = total.astype(jnp.bfloat16)
        image[o] = out
        out = out.astype(jnp.float32)
        squares += jnp.sum((out * out).reshape(-1, 8, width), axis=0)
    partial[...] = sum(squares[:, lane : lane + 128] for lane in range(0, width, 128))


def second_kernel(blocks, terms, own, image, keep, mine, *refs):
    lefts, rights, (final, raw, products) = refs[:terms], refs[terms:-3], refs[-3:]
    final[0] = image[...]
    for o, total in enumerate(apply_tiles(blocks, terms, own, image, keep, mine, lefts, rights, products)):
        raw[0, o] = total


def scale_kernel(count, raw, norm, other, image):
    norm_sum = jnp.sum(norm[...] + other[...])
    image[...] = (raw[...] * lax.rsqrt(norm_sum / count + 1e-06)).astype(jnp.bfloat16)


def cost(dots, width):
    return pl.CostEstimate(flops=dots * 2 * width**3, bytes_accessed=8 * width**2, transcendentals=0)


def local(blocks, terms, two_site, left_env, right_env, row_size, col_size, block_live):
    width = two_site.shape[2]
    n_cols = two_site.shape[1]
    own = n_cols // terms
    vmem, hbm = pl.BlockSpec(memory_space=pltpu.VMEM), pl.BlockSpec(memory_space=pltpu.HBM)
    params = pltpu.CompilerParams(vmem_limit_bytes=32 * 1024 * 1024)
    everyone = [(a, t) for a in range(blocks) for t in range(terms)]

    rights = [move(right_env, pairs, terms) for pairs in right_routes(blocks, terms, own)]
    lefts = [left_env] + [None] * (terms - 1)
    for m in list(range(3, terms, 2)) + list(range(2, terms, 2)) + [1]:
        source, hop = (left_env, m) if m % 2 else (lefts[m + 1], 1)
        if m == 1:
            source, _ = lax.optimization_barrier((left_env, rights[-1]))
        lefts[m] = move(source, [((a, t), (a, t ^ hop)) for a, t in everyone], terms)

    tile = (own, width, width)
    start, keep = pl.pallas_call(
        functools.partial(start_kernel, own),
        out_shape=(
            jax.ShapeDtypeStruct(tile, jnp.bfloat16),
            jax.ShapeDtypeStruct(tile, jnp.float32),
        ),
        in_specs=[hbm] * 4,
        out_specs=(vmem,) * 2,
        scratch_shapes=[
            pltpu.VMEM(tile, jnp.bfloat16),
            pltpu.SMEM(row_size.shape, jnp.int32),
            pltpu.SMEM(col_size.shape, jnp.int32),
            pltpu.SMEM(block_live.shape, jnp.int32),
            pltpu.SemaphoreType.DMA((4,)),
        ],
        compiler_params=params,
        cost_estimate=cost(0, width),
    )(two_site, row_size, col_size, block_live)

    def apply_call(kernel, operand, outs):
        return pl.pallas_call(
            functools.partial(kernel, blocks, terms, own),
            out_shape=outs,
            in_specs=[vmem] * (3 + terms + blocks),
            out_specs=(vmem,) * 2,
            scratch_shapes=[pltpu.VMEM((blocks, width, width), jnp.bfloat16)],
            compiler_params=params,
            cost_estimate=cost(2 * blocks, width),
        )(operand, keep, right_env, *lefts, *rights)

    first, partial = apply_call(
        first_kernel,
        start,
        (jax.ShapeDtypeStruct(tile, jnp.bfloat16), jax.ShapeDtypeStruct((8, 128), jnp.float32)),
    )
    first_image, raw = apply_call(
        second_kernel,
        first,
        (jax.ShapeDtypeStruct((1,) + tile, jnp.bfloat16), jax.ShapeDtypeStruct((1,) + tile, jnp.float32)),
    )

    flips = [(0, 1)] + [(0, 1 | 1 << s) for s in range(1, (terms - 1).bit_length())]
    flips += [(1 << s, 1) for s in range((blocks - 1).bit_length())]
    if len(flips) == 4:
        flips = [flips[i] for i in (1, 3, 0, 2)]
    norm, other = partial, None
    for da, dt in flips:
        norm = norm if other is None else norm + other
        other = move(norm, [((a, t), (a ^ da, t ^ dt)) for a, t in everyone], terms)

    second_image = pl.pallas_call(
        functools.partial(scale_kernel, float(blocks * n_cols * width * width)),
        out_shape=jax.ShapeDtypeStruct((1,) + tile, jnp.bfloat16),
        in_specs=[vmem] * 3,
        out_specs=vmem,
        compiler_params=params,
    )(raw, norm, other)
    return first_image, second_image


def solution(mesh):
    return jax.shard_map(
        functools.partial(local, mesh.shape["blk"], mesh.shape["term"]),
        mesh=mesh,
        in_specs=(
            P(("runs", "blk"), None, None, None),
            P(("runs", "term"), "blk", None, None),
            P(("runs", "term"), "blk", None, None),
            P(("runs", "blk")),
            P("runs"),
            P(("runs", "blk"), None),
        ),
        out_specs=(P(("runs", "blk"), "term", None, None), P(("runs", "blk"), "term", None, None)),
        check_vma=False,
    )
```

```python
import functools

import jax
import jax.numpy as jnp
from jax import lax
from jax.experimental import pallas as pl
from jax.experimental.pallas import tpu as pltpu
from jax.sharding import PartitionSpec as P

AXES = ("blk", "term")


def move(value, pairs, terms):
    return lax.ppermute(
        value, AXES, [(a * terms + b, c * terms + d) for (a, b), (c, d) in pairs]
    )


ROUTES = (
    ((0, 2, 3, 1), (3, 1, 0, 2), (1, 3, 2, 0), (2, 0, 1, 3)),
    ((3, 1, 2, 0), (1, 3, 0, 2), (2, 0, 3, 1), (0, 2, 1, 3)),
    ((3, 1, 2, 0), (1, 3, 0, 2), (0, 2, 1, 3), (2, 0, 3, 1)),
    ((0, 2, 1, 3), (2, 0, 3, 1), (1, 3, 0, 2), (3, 1, 2, 0)),
)


def source_number(blocks, own, blk, term, step):
    if blocks == 4 and own == 1:
        packed = sum(i << (8 * g + 2 * p) for g, r in enumerate(ROUTES) for i, p in enumerate(r[step]))
        if not isinstance(blk, int):
            packed = jnp.int32(packed - (packed >> 31 << 32))
        return (packed >> (8 * term + 2 * blk)) & 3
    half, place = blocks // 2, blk ^ step
    return (place % half) * 2 + place // half


def right_routes(blocks, terms, own):
    routes = []
    for step in range(blocks):
        pairs = []
        for a in range(blocks):
            for group in range(terms):
                i = source_number(blocks, own, a, group, step)
                source = (group * own + i // terms, i % terms)
                if source != (a, group):
                    pairs.append((source, (a, group)))
        routes.append(pairs)
    return routes


def dot(a, b):
    return jnp.dot(a, b, preferred_element_type=jnp.float32)


def start_kernel(own, two_site, rows, cols, live, start, keep, tiles, rows_at, cols_at, live_at, sems):
    term = lax.axis_index("term")
    width = tiles.shape[-1]
    copies = [
        pltpu.make_async_copy(two_site.at[0, pl.ds(term * own, own)], tiles, sems.at[0]),
        pltpu.make_async_copy(rows, rows_at, sems.at[1]),
        pltpu.make_async_copy(cols, cols_at, sems.at[2]),
        pltpu.make_async_copy(live, live_at, sems.at[3]),
    ]
    for copy in copies:
        copy.start()
    for copy in copies:
        copy.wait()
    at_row = lax.broadcasted_iota(jnp.int32, (width, width), 0)
    at_col = lax.broadcasted_iota(jnp.int32, (width, width), 1)
    for o in range(own):
        col = term * own + o
        mask = (at_row < rows_at[0]) & (at_col < cols_at[col]) & (live_at[0, col] == 1)
        start[o] = jnp.where(mask, tiles[o], jnp.zeros((), tiles.dtype))
        keep[o] = jnp.where(mask, 1.0, 0.0)


def apply_tiles(blocks, terms, own, tile, keep, mine, lefts, rights, products):
    blk, term = lax.axis_index("blk"), lax.axis_index("term")
    for step, right in enumerate(rights):
        i = source_number(blocks, own, blk, term, step)
        products[i] = dot(tile[i // terms], right[0, 0]).astype(jnp.bfloat16)

    @pl.when(blk // own == term)
    def _():
        o = blk % own
        products[o * terms + term] = dot(tile[o], mine[0, 0]).astype(jnp.bfloat16)

    sums = []
    for o in range(own):
        wide = jnp.concatenate([left[0, 0] for left in lefts], axis=1)
        tall = jnp.concatenate([products[o * terms + (term ^ m)] for m in range(terms)], axis=0)
        total = dot(wide, tall)
        sums.append(jnp.where(keep[o] != 0.0, total, 0.0))
    return sums


def first_kernel(blocks, terms, own, start, keep, mine, *refs):
    lefts, rights, (image, partial, products) = refs[:terms], refs[terms:-3], refs[-3:]
    width = start.shape[-1]
    squares = jnp.zeros((8, width), jnp.float32)
    for o, total in enumerate(apply_tiles(blocks, terms, own, start, keep, mine, lefts, rights, products)):
        out = total.astype(jnp.bfloat16)
        image[o] = out
        out = out.astype(jnp.float32)
        squares += jnp.sum((out * out).reshape(-1, 8, width), axis=0)
    partial[...] = sum(squares[:, lane : lane + 128] for lane in range(0, width, 128))


def second_kernel(blocks, terms, own, image, keep, mine, *refs):
    lefts, rights, (final, raw, products) = refs[:terms], refs[terms:-3], refs[-3:]
    final[0] = image[...]
    for o, total in enumerate(apply_tiles(blocks, terms, own, image, keep, mine, lefts, rights, products)):
        raw[0, o] = total


def scale_kernel(count, raw, norm, other, image):
    norm_sum = jnp.sum(norm[...] + other[...])
    image[...] = (raw[...] * lax.rsqrt(norm_sum / count + 1e-06)).astype(jnp.bfloat16)


def cost(dots, width):
    return pl.CostEstimate(flops=dots * 2 * width**3, bytes_accessed=8 * width**2, transcendentals=0)


def local(blocks, terms, two_site, left_env, right_env, row_size, col_size, block_live):
    width = two_site.shape[2]
    n_cols = two_site.shape[1]
    own = n_cols // terms
    vmem, hbm = pl.BlockSpec(memory_space=pltpu.VMEM), pl.BlockSpec(memory_space=pltpu.HBM)
    params = pltpu.CompilerParams(vmem_limit_bytes=32 * 1024 * 1024)
    everyone = [(a, t) for a in range(blocks) for t in range(terms)]

    rights = [move(right_env, pairs, terms) for pairs in right_routes(blocks, terms, own)]
    lefts = [left_env] + [None] * (terms - 1)
    for m in list(range(3, terms, 2)) + list(range(2, terms, 2)) + [1]:
        source, hop = (left_env, m) if m % 2 else (lefts[m + 1], 1)
        if m == 1:
            source, _ = lax.optimization_barrier((left_env, rights[-1]))
        lefts[m] = move(source, [((a, t), (a, t ^ hop)) for a, t in everyone], terms)

    tile = (own, width, width)
    start, keep = pl.pallas_call(
        functools.partial(start_kernel, own),
        out_shape=(
            jax.ShapeDtypeStruct(tile, jnp.bfloat16),
            jax.ShapeDtypeStruct(tile, jnp.float32),
        ),
        in_specs=[hbm] * 4,
        out_specs=(vmem,) * 2,
        scratch_shapes=[
            pltpu.VMEM(tile, jnp.bfloat16),
            pltpu.SMEM(row_size.shape, jnp.int32),
            pltpu.SMEM(col_size.shape, jnp.int32),
            pltpu.SMEM(block_live.shape, jnp.int32),
            pltpu.SemaphoreType.DMA((4,)),
        ],
        compiler_params=params,
        cost_estimate=cost(0, width),
    )(two_site, row_size, col_size, block_live)

    def apply_call(kernel, operand, outs):
        return pl.pallas_call(
            functools.partial(kernel, blocks, terms, own),
            out_shape=outs,
            in_specs=[vmem] * (3 + terms + blocks),
            out_specs=(vmem,) * 2,
            scratch_shapes=[pltpu.VMEM((blocks, width, width), jnp.bfloat16)],
            compiler_params=params,
            cost_estimate=cost(2 * blocks, width),
        )(operand, keep, right_env, *lefts, *rights)

    first, partial = apply_call(
        first_kernel,
        start,
        (jax.ShapeDtypeStruct(tile, jnp.bfloat16), jax.ShapeDtypeStruct((8, 128), jnp.float32)),
    )
    first_image, raw = apply_call(
        second_kernel,
        first,
        (jax.ShapeDtypeStruct((1,) + tile, jnp.bfloat16), jax.ShapeDtypeStruct((1,) + tile, jnp.float32)),
    )

    flips = [(0, 1)] + [(0, 1 | 1 << s) for s in range(1, (terms - 1).bit_length())]
    flips += [(1 << s, 1) for s in range((blocks - 1).bit_length())]
    if len(flips) == 4:
        flips = [flips[i] for i in (1, 3, 0, 2)]
    norm, other = partial, None
    for da, dt in flips:
        norm = norm if other is None else norm + other
        other = move(norm, [((a, t), (a ^ da, t ^ dt)) for a, t in everyone], terms)

    second_image = pl.pallas_call(
        functools.partial(scale_kernel, float(blocks * n_cols * width * width)),
        out_shape=jax.ShapeDtypeStruct((1,) + tile, jnp.bfloat16),
        in_specs=[vmem] * 3,
        out_specs=vmem,
        compiler_params=params,
    )(raw, norm, other)
    return first_image, second_image


def solution(mesh):
    return jax.shard_map(
        functools.partial(local, mesh.shape["blk"], mesh.shape["term"]),
        mesh=mesh,
        in_specs=(
            P(("runs", "blk"), None, None, None),
            P(("runs", "term"), "blk", None, None),
            P(("runs", "term"), "blk", None, None),
            P(("runs", "blk")),
            P("runs"),
            P(("runs", "blk"), None),
        ),
        out_specs=(P(("runs", "blk"), "term", None, None), P(("runs", "blk"), "term", None, None)),
        check_vma=False,
    )
```
